256 devices in a mesh: row: 8 (over y, x_lo), col: 32 (over x_hi, z, core).
Axes of the slice: x: 4 (x_hi: 2, x_lo: 2; x = x_hi * 2 + x_lo), y: 4, z: 8, core: 2. Of those that a mesh axis runs over, the one named last changes fastest.
Arguments:
- embeddings: float32 [24576, 1024], P(('col', 'row')), may hold values from -8 to 8
Outputs:
- smoothed: float32 [24576, 1024], P(('col', 'row'))
- log_density: float32 [24576], P(('col', 'row'))
The draws below stay inside these ranges and needn't reach their ends.
All inputs are finite; a program needn't handle non-finite values.
Results may differ from the reference program's by a relative error of at most 0.022.
Values may be sent and summed in bfloat16 or wider, within the bound.
No kernel may reach another device: no remote copies, remote signals or barrier semaphores. Data moves between devices by JAX's collectives and lax.ppermute only.
A program may use at most 64 MiB of HBM per device.

```python
import math
import jax
import jax.numpy as jnp
from jax import lax

D = 1024
N = 24576


def shared_factors(key, loading_scale):
    factors = jax.random.normal(jax.random.fold_in(key, 11), (N, 8), jnp.float32)
    loadings = jax.random.normal(jax.random.fold_in(key, 12), (8, D), jnp.float32) * loading_scale
    summed = jnp.zeros((N, D), jnp.float32)
    for index in range(8):
        summed = summed + factors[:, index:index + 1] * loadings[index:index + 1, :]
    return summed


def draw_embeddings(key, part):
    key = jax.random.fold_in(key, 7)
    common = shared_factors(key, 0.5)
    base = jnp.clip(jax.random.normal(jax.random.fold_in(key, 1), (N, D), jnp.float32), -6.0, 6.0)
    return jnp.clip(base + common, -8.0, 8.0)


def setup_inputs(seed: int = 0) -> dict:
    keys = jax.random.split(jax.random.key(seed), 2)
    embeddings = draw_embeddings(jax.random.fold_in(keys[1], 71), 0)
    return dict(embeddings=embeddings)


SHARPNESS = 24.0

def reference(embeddings):
    count = embeddings.shape[0]
    width = embeddings.shape[1]
    first = jnp.sum(embeddings, axis=0)
    second = jnp.dot(embeddings.T.astype(jnp.float32), embeddings.astype(jnp.float32), precision=lax.Precision.HIGHEST, preferred_element_type=jnp.float32)
    mean = first / count
    cov = second / count - jnp.outer(mean, mean)
    chol = jnp.linalg.cholesky(cov)
    centred = embeddings - mean[None, :]
    white = lax.linalg.triangular_solve(chol, centred, left_side=False, lower=True, transpose_a=True).astype(jnp.bfloat16)
    white_f = white.astype(jnp.float32)
    squares = jnp.sum(white_f * white_f, axis=1)
    block = math.gcd(count, 512)
    nblocks = count // block
    key_index = jnp.arange(count, dtype=jnp.int32)

    def one_block(index):
        begin = (index * block).astype(jnp.int32)
        queries = lax.dynamic_slice_in_dim(white, begin, block, 0)
        q_squares = lax.dynamic_slice_in_dim(squares, begin, block, 0)
        dots = jnp.dot(queries.astype(jnp.float32), white.T.astype(jnp.float32), preferred_element_type=jnp.float32)
        expo = SHARPNESS * (2.0 - (q_squares[:, None] + squares[None, :] - 2.0 * dots) / width)
        query_index = begin + jnp.arange(block, dtype=jnp.int32)
        kern = jnp.where(query_index[:, None] == key_index[None, :], 0.0, jnp.exp(expo))
        total = jnp.sum(kern, axis=1)
        numer = jnp.dot(kern.astype(jnp.bfloat16).astype(jnp.float32), white.astype(jnp.float32), preferred_element_type=jnp.float32)
        return (numer / total[:, None], jnp.log(total / (count - 1)))
    smooth, logs = lax.map(one_block, jnp.arange(nblocks, dtype=jnp.int32))
    return (smooth.reshape(count, width), logs.reshape(count))
```

```python
import functools
import math
import jax
import jax.numpy as jnp
from jax import lax
from jax.experimental import pallas as pl
from jax.experimental.pallas import tpu as pltpu
from jax.sharding import PartitionSpec as P

SHARPNESS = 24.0
BLOCK = 128
PANEL = 16
EXTRA = 128
VMEM = 56 * 2**20
AXES = ("row", "col")
NN = ((1,), (0,))
NT = ((1,), (1,))
BF16 = jnp.bfloat16
F32 = jnp.float32


def split(a):
    hi = a.astype(BF16)
    return hi, (a - hi.astype(F32)).astype(BF16)


def mul(a, b, dims):
    return lax.dot_general(a, b, (dims, ((), ())), preferred_element_type=F32)


def dot3(a, b, dims):
    a_hi, a_lo = split(a)
    b_hi, b_lo = split(b)
    return mul(a_hi, b_hi, dims) + (mul(a_hi, b_lo, dims) + mul(a_lo, b_hi, dims))


def iota(shape, dim):
    return lax.broadcasted_iota(jnp.int32, shape, dim)


def moments_kernel(core_ref, x_ref, keep_ref, send_ref, packed):
    rows, width = x_ref.shape
    half = width // 2
    x = jnp.concatenate([x_ref[...], jnp.zeros((BLOCK - rows, width), F32)], 0)
    hi, lo = split(x)
    xt = jnp.concatenate([x[:, c : c + BLOCK].T for c in range(0, width, BLOCK)], 0)
    xt_hi, xt_lo = split(xt)
    left = jnp.concatenate([xt_hi, xt_lo], 1)
    ones = jnp.where(iota((BLOCK, EXTRA), 1) == 0, 1.0, 0.0).astype(BF16)
    none = jnp.zeros((BLOCK, EXTRA), BF16)
    one = jnp.concatenate([jnp.concatenate([hi, ones], 1), jnp.concatenate([lo, ones], 1)], 0)
    two = jnp.concatenate([jnp.concatenate([lo, none], 1), jnp.concatenate([hi, none], 1)], 0)
    low = mul(left[half:], one, NN) + mul(left[half:], two, NN)
    up = mul(left[:half], one[:, :half], NN) + mul(left[:half], two[:, :half], NN)
    up_sum = mul(left[:half], one[:, width:], NN)
    r, c = iota((half, half), 0), iota((half, half), 1)
    diag = jnp.sum(jnp.where(r == c, up, 0.0), axis=1, keepdims=True)
    lane = iota((half, EXTRA), 1)
    packed[:, :half] = low[:, :half]
    packed[:, half:width] = jnp.where(r >= c, low[:, half:width], up)
    packed[:, width:] = jnp.where(
        lane == 0,
        low[:, width:],
        jnp.where(lane == 1, up_sum[:, :1], jnp.where(lane == 2, diag, 0.0)),
    )
    part = half // 2
    core = core_ref[0]
    keep_ref[...] = packed[pl.ds(pl.multiple_of(core * part, part), part), :]
    send_ref[...] = packed[pl.ds(pl.multiple_of((1 - core) * part, part), part), :]


def moments(core, x):
    width = x.shape[1]
    half = width // 2
    out = jax.ShapeDtypeStruct((half // 2, width + EXTRA), F32)
    return pl.pallas_call(
        moments_kernel,
        out_shape=(out, out),
        in_specs=[
            pl.BlockSpec(memory_space=pltpu.SMEM),
            pl.BlockSpec(memory_space=pltpu.VMEM),
        ],
        out_specs=(pl.BlockSpec(memory_space=pltpu.VMEM),) * 2,
        scratch_shapes=[pltpu.VMEM((half, width + EXTRA), F32)],
        compiler_params=pltpu.CompilerParams(vmem_limit_bytes=VMEM),
        name="moments",
    )(core, x)


def diag_factor(g, w):
    lane = iota((PANEL, BLOCK), 1)
    sub = iota((PANEL, BLOCK), 0)
    for o in range(0, BLOCK, PANEL):
        r = g[o : o + PANEL, :]
        cols = [jnp.broadcast_to(r[:, o + s : o + s + 1], r.shape) for s in range(PANEL)]
        inside = (lane >= o) & (lane < o + PANEL)
        e = jnp.where(inside, jnp.where(lane - o == sub, 1.0, 0.0), r)
        y = jnp.zeros_like(r)
        for s in range(PANEL):
            d = jnp.broadcast_to(cols[s][s : s + 1, :], r.shape)
            inv = 1.0 / d
            m = cols[s] * inv
            pivot = jnp.broadcast_to(e[s : s + 1, :], r.shape)
            y = jnp.where(sub == s, pivot * lax.rsqrt(d), y)
            e = jnp.where(sub != s, e - m * pivot, pivot * inv)
            for t in range(s + 1, PANEL):
                c = jnp.broadcast_to(cols[t][s : s + 1, :], r.shape)
                cols[t] = jnp.where(sub != s, cols[t] - m * c, c * inv)
        w[o : o + PANEL, :] = jnp.where(lane <= sub + o, y, 0.0)
        after = o + PANEL
        if after < BLOCK:
            rest = g[after:, :]
            place = iota(rest.shape, 1)
            inside = (place >= o) & (place < after)
            parts = [e, jnp.zeros((BLOCK - after, BLOCK), F32)]
            if o:
                parts = [jnp.zeros((o, BLOCK), F32)] + parts
            z = jnp.concatenate(parts, 0)
            g[after:, :] = jnp.where(inside, 0.0, rest) - dot3(jnp.where(inside, rest, 0.0), z, NN)


def whiten_kernel(count, core_ref, mine_ref, other_ref, x_ref, white_ref, packed, m, w, g, wd):
    width = x_ref.shape[1]
    half = width // 2
    part = half // 2
    core = core_ref[0]
    scale = 1.0 / count
    packed[pl.ds(pl.multiple_of(core * part, part), part), :] = mine_ref[...] * scale
    packed[pl.ds(pl.multiple_of((1 - core) * part, part), part), :] = other_ref[...] * scale
    tail = packed[:, width:]
    tail_t = tail.T
    low_col, up_col, diag = tail[:, 0:1], tail[:, 1:2], tail[:, 2:3]
    low_row, up_row = tail_t[0:1, :], tail_t[1:2, :]
    m[half:, :half] = packed[:, :half] - low_col * up_row
    right = packed[:, half:width]
    low = right - low_col * low_row
    up = jnp.where(iota((half, half), 0) == iota((half, half), 1), diag, right) - up_col * up_row
    for i in range(0, half, BLOCK):
        keep = iota((BLOCK, BLOCK), 0) >= iota((BLOCK, BLOCK), 1)
        for j in range(0, i + BLOCK, BLOCK):
            block = up[j : j + BLOCK, i : i + BLOCK]
            turned = block.T
            if i == j:
                turned = jnp.where(keep, turned, block)
            m[i : i + BLOCK, j : j + BLOCK] = turned
            block = low[i : i + BLOCK, j : j + BLOCK]
            if i == j:
                block = jnp.where(keep, block, block.T)
            m[half + i : half + i + BLOCK, half + j : half + j + BLOCK] = block
    for b in range(0, width, BLOCK):
        after = b + BLOCK
        g[...] = m[b:after, b:after]
        diag_factor(g, wd)
        wk = wd[...]
        w[b:after, b:after] = wk
        if b:
            w[b:after, :b] = dot3(wk, m[b:after, :b], NN)
        if after < width:
            lk = dot3(m[after:, b:after], wk, NT)
            m[after:, b:after] = jnp.zeros((width - after, BLOCK), F32)
            m[after:, :after] = m[after:, :after] - dot3(lk, w[b:after, :after], NN)
            m[after:, after:] = m[after:, after:] - dot3(lk, lk, NT)
    mean = jnp.concatenate([up_row, low_row], 1)
    centred = x_ref[...] - mean
    step = 256
    for j in range(0, width, step):
        if j + step < width:
            w[j : j + BLOCK, j + BLOCK : j + step] = jnp.zeros((BLOCK, step - BLOCK), F32)
        else:
            w[j : j + BLOCK, j + BLOCK :] = jnp.zeros((BLOCK, width - j - BLOCK), F32)
        white_ref[:, j : j + step] = dot3(
            centred[:, : j + step], w[j : j + step, : j + step], NT
        ).astype(BF16)


def whiten(count, core, mine, other, x):
    width = x.shape[1]
    half = width // 2
    vmem = pl.BlockSpec(memory_space=pltpu.VMEM)
    return pl.pallas_call(
        functools.partial(whiten_kernel, count),
        out_shape=jax.ShapeDtypeStruct(x.shape, BF16),
        in_specs=[pl.BlockSpec(memory_space=pltpu.SMEM), vmem, vmem, vmem],
        out_specs=vmem,
        scratch_shapes=[
            pltpu.VMEM((half, width + EXTRA), F32),
            pltpu.VMEM((width, width), F32),
            pltpu.VMEM((width, width), F32),
            pltpu.VMEM((BLOCK, BLOCK), F32),
            pltpu.VMEM((BLOCK, BLOCK), F32),
        ],
        compiler_params=pltpu.CompilerParams(vmem_limit_bytes=VMEM),
        name="whiten",
    )(core, mine, other, x)


def terms_kernel(rows, row_ref, q_ref, *refs):
    key_refs, out_ref, keys, numer = refs[:-3], refs[-3], refs[-2], refs[-1]
    queries, width = q_ref.shape
    rate = SHARPNESS / width * math.log2(math.e)
    q = q_ref[...]
    qf = q.astype(F32)
    q_term = 2.0 * SHARPNESS * math.log2(math.e) - rate * jnp.sum(qf * qf, axis=1, keepdims=True)
    total = jnp.zeros((queries, 1), F32)
    chunk = keys.shape[0]
    place = 0
    done = 0
    total_rows = sum(ref.shape[0] for ref in key_refs)
    for ref in key_refs:
        size = ref.shape[0]
        keys[place : place + size, :] = ref[...]
        place += size
        if place < chunk and done + place < total_rows:
            continue
        k = keys[:place, :]
        kf = k.astype(F32)
        k_sq = jnp.sum(kf * kf, axis=1, keepdims=True)
        k_row = jnp.concatenate(
            [jnp.broadcast_to(k_sq[j : j + 128], (128, 128)).T[0:1, :] for j in range(0, place, 128)], 1
        )
        kern = jnp.exp2(q_term - rate * k_row + (2.0 * rate) * mul(q, k, NT))
        if done == 0:
            own = (iota(kern.shape, 0) - row_ref[0] * rows == iota(kern.shape, 1)) & (
                iota(kern.shape, 1) < rows
            )
            kern = jnp.where(own, 0.0, kern)
        total = total + jnp.sum(kern, axis=1, keepdims=True)
        term = mul(kern.astype(BF16), k, NN)
        if done == 0:
            numer[...] = term
        else:
            numer[...] += term
        done += place
        place = 0
    out_ref[:, :width] = numer[...].astype(BF16)
    hi, lo = split(total)
    lane = iota((queries, EXTRA), 1)
    wide = jnp.where(lane == 0, hi.astype(F32), jnp.where(lane == 1, lo.astype(F32), 0.0))
    out_ref[:, width:] = wide.astype(BF16)


def terms(row, rows, q, key_list, chunk):
    queries, width = q.shape
    vmem = pl.BlockSpec(memory_space=pltpu.VMEM)
    return pl.pallas_call(
        functools.partial(terms_kernel, rows),
        out_shape=jax.ShapeDtypeStruct((queries, width + EXTRA), BF16),
        in_specs=[pl.BlockSpec(memory_space=pltpu.SMEM)] + [vmem] * (1 + len(key_list)),
        out_specs=vmem,
        scratch_shapes=[pltpu.VMEM((chunk, width), BF16), pltpu.VMEM((queries, width), F32)],
        compiler_params=pltpu.CompilerParams(vmem_limit_bytes=VMEM),
        name="terms",
    )(row, q, *key_list)


def shift(sizes, dx=0, dz=0, dc=0):
    rows, his, zs = sizes
    pairs = []
    for r in range(rows):
        for h in range(his):
            for z in range(zs):
                for c in range(2):
                    src = ((r * his + h) * zs + z) * 2 + c
                    dst = ((r * his + (h + dx) % his) * zs + (z + dz) % zs) * 2 + (c ^ dc)
                    pairs.append((src, dst))
    return pairs


def shards(embeddings):
    rows, width = embeddings.shape
    row_count = lax.axis_size("row")
    col_count = lax.axis_size("col")
    count = rows * row_count * col_count
    row_pos = lax.axis_index("row")
    core = (lax.axis_index("col") % 2).astype(jnp.int32)[None]
    row = row_pos.astype(jnp.int32)[None]
    his, zs = 2, col_count // 4
    sizes = (row_count, his, zs)
    half = col_count // 2
    groups = [[2 * i + c for i in range(half)] for c in range(2)]
    send = functools.partial(lax.ppermute, axis_name=AXES)
    to_core = shift(sizes, dc=1)

    keep, give = moments(core, embeddings)
    mine = keep + send(give, perm=to_core)
    wide = mine.shape[1]
    mine = lax.all_to_all(mine.reshape(row_count, -1, wide), "row", 0, 0).sum(0)
    mine = lax.all_to_all(
        mine.reshape(half, -1, wide), "col", 0, 0, axis_index_groups=groups
    ).sum(0)
    mine = lax.all_to_all(
        jnp.broadcast_to(mine[None], (half,) + mine.shape), "col", 0, 0, axis_index_groups=groups
    ).reshape(-1, wide)
    mine = lax.all_to_all(
        jnp.broadcast_to(mine[None], (row_count,) + mine.shape), "row", 0, 0
    ).reshape(-1, wide)
    other = send(mine, perm=to_core)
    white = whiten(count, core, mine, other, embeddings)

    queries = lax.all_to_all(
        jnp.broadcast_to(white[None], (row_count, rows, width)), "row", 0, 0
    ).reshape(row_count * rows, width)
    far = send(white, perm=shift(sizes, dx=1))
    pair = jnp.concatenate([white, far], 0)
    held = [pair]
    right = left = pair
    up, down = shift(sizes, dz=1), shift(sizes, dz=-1)
    for _ in range((zs - 1) // 2):
        right = send(right, perm=up)
        left = send(left, perm=down)
        held += [right, left]
    if zs % 2 == 0:
        held += [send(right[:rows], perm=up), send(left[rows:], perm=down)]
    held += [send(block, perm=to_core) for block in held]
    partial = terms(row, rows, queries, held, 768)
    parts = lax.all_to_all(partial.reshape(row_count, rows, -1), "row", 0, 0)
    sums = jnp.sum(parts.astype(F32), axis=0)
    total = sums[:, width] + sums[:, width + 1]
    smoothed = sums[:, :width] / total[:, None]
    log_density = jnp.log(total / (count - 1))
    return (smoothed, log_density)


def solution(mesh):
    in_specs = (P(("col", "row"), None),)
    out_specs = (P(("col", "row"), None), P(("col", "row")))
    return jax.shard_map(shards, mesh=mesh, in_specs=in_specs, out_specs=out_specs, check_vma=False)
```

```python
import functools
import math
import jax
import jax.numpy as jnp
from jax import lax
from jax.experimental import pallas as pl
from jax.experimental.pallas import tpu as pltpu
from jax.sharding import PartitionSpec as P

SHARPNESS = 24.0
BLOCK = 128
PANEL = 16
EXTRA = 128
VMEM = 56 * 2**20
TERMS_VMEM = 40 * 2**20
AXES = ("row", "col")
NN = ((1,), (0,))
NT = ((1,), (1,))
BF16 = jnp.bfloat16
F32 = jnp.float32


def split(a):
    hi = a.astype(BF16)
    return hi, (a - hi.astype(F32)).astype(BF16)


def mul(a, b, dims):
    return lax.dot_general(a, b, (dims, ((), ())), preferred_element_type=F32)


def dot3(a, b, dims):
    a_hi, a_lo = split(a)
    b_hi, b_lo = split(b)
    return mul(a_hi, b_hi, dims) + (mul(a_hi, b_lo, dims) + mul(a_lo, b_hi, dims))


def iota(shape, dim):
    return lax.broadcasted_iota(jnp.int32, shape, dim)


def moments_kernel(core_ref, x_ref, y_ref, out_ref, turned_hi, turned_lo):
    rows, width = x_ref.shape
    half = width // 2
    part = half // 2
    pad = jnp.zeros((BLOCK - rows, width), F32)
    x = jnp.concatenate([x_ref[...], pad, y_ref[...], pad], 0)
    hi, lo = split(x)
    for c in range(0, width, BLOCK):
        t_hi, t_lo = split(x[:, c : c + BLOCK].T)
        turned_hi[c : c + BLOCK, :] = t_hi
        turned_lo[c : c + BLOCK, :] = t_lo
    core = core_ref[0]

    def product(start, right_hi, right_lo):
        place = pl.ds(pl.multiple_of(start + core * part, part), part)
        left_hi, left_lo = turned_hi[place, :], turned_lo[place, :]
        small = mul(left_lo, right_lo, NN)
        small = small + (mul(left_hi, right_lo, NN) + mul(left_lo, right_hi, NN))
        return mul(left_hi, right_hi, NN) + small

    low = product(half, hi, lo)
    up = product(0, hi[:, :half], lo[:, :half])
    ones = jnp.where(iota((2 * BLOCK, EXTRA), 1) == 0, 1.0, 0.0).astype(BF16)
    none = jnp.zeros((2 * BLOCK, EXTRA), BF16)
    low_sum = product(half, ones, none)
    up_sum = product(0, ones, none)
    r, c = iota((part, half), 0) + core * part, iota((part, half), 1)
    diag = jnp.sum(jnp.where(r == c, up, 0.0), axis=1, keepdims=True)
    lane = iota((part, EXTRA), 1)
    out_ref[:, :half] = low[:, :half]
    out_ref[:, half:width] = jnp.where(r >= c, low[:, half:], up)
    out_ref[:, width:] = jnp.where(
        lane == 0,
        low_sum,
        jnp.where(lane == 1, up_sum[:, :1], jnp.where(lane == 2, diag, 0.0)),
    )


def moments(core, x, y):
    width = x.shape[1]
    vmem = pl.BlockSpec(memory_space=pltpu.VMEM)
    return pl.pallas_call(
        moments_kernel,
        out_shape=jax.ShapeDtypeStruct((width // 4, width + EXTRA), F32),
        in_specs=[pl.BlockSpec(memory_space=pltpu.SMEM), vmem, vmem],
        out_specs=vmem,
        scratch_shapes=[pltpu.VMEM((width, 2 * BLOCK), BF16)] * 2,
        compiler_params=pltpu.CompilerParams(vmem_limit_bytes=VMEM),
        name="moments",
    )(core, x, y)


def row_of(v, s):
    return jnp.broadcast_to(v[s : s + 1, :], (PANEL, BLOCK))


def columns_of(v, o):
    return [jnp.broadcast_to(v[:, o + s : o + s + 1], (PANEL, BLOCK)) for s in range(PANEL)]


def diag_factor(g, w):
    lane = iota((PANEL, BLOCK), 1)
    sub = iota((PANEL, BLOCK), 0)
    r = g[:PANEL, :]
    for o in range(0, BLOCK, PANEL):
        after = o + PANEL
        if after < BLOCK:
            ahead = g[after : after + PANEL, :]
            factors = columns_of(ahead, o)
        cols = columns_of(r, o)
        inside = (lane >= o) & (lane < after)
        e = jnp.where(inside, jnp.where(lane - o == sub, 1.0, 0.0), r)
        y = jnp.zeros_like(r)
        for s in range(PANEL):
            d = row_of(cols[s], s)
            inv = 1.0 / d
            pivot = row_of(e, s)
            y = jnp.where(sub == s, pivot * lax.rsqrt(d), y)
            m = jnp.where(sub != s, cols[s] * inv, 1.0 - inv)
            e = e - m * pivot
            for t in range(s + 1, PANEL):
                cols[t] = cols[t] - m * row_of(cols[t], s)
        w[o:after, :] = jnp.where(lane <= sub + o, y, 0.0)
        if after < BLOCK:
            sums = [jnp.zeros_like(r)] * 4
            for s in range(PANEL):
                sums[s % 4] = sums[s % 4] + factors[s] * row_of(e, s)
            r = jnp.where(inside, 0.0, ahead) - ((sums[0] + sums[1]) + (sums[2] + sums[3]))
        far = after + PANEL
        if far < BLOCK:
            rest = g[far:, :]
            place = iota(rest.shape, 1)
            inside = (place >= o) & (place < after)
            parts = [e, jnp.zeros((BLOCK - after, BLOCK), F32)]
            if o:
                parts = [jnp.zeros((o, BLOCK), F32)] + parts
            z = jnp.concatenate(parts, 0)
            g[far:, :] = jnp.where(inside, 0.0, rest) - dot3(jnp.where(inside, rest, 0.0), z, NN)


def whiten_kernel(
    count, core_ref, mine_ref, other_ref, x_ref, white_ref, packed, m, w, g, wd
):
    width = x_ref.shape[1]
    half = width // 2
    part = half // 2
    core = core_ref[0]
    scale = 1.0 / count
    packed[pl.ds(pl.multiple_of(core * part, part), part), :] = mine_ref[...] * scale
    packed[pl.ds(pl.multiple_of((1 - core) * part, part), part), :] = other_ref[...] * scale
    tail = packed[:, width:]
    tail_t = tail.T
    low_col, up_col, diag = tail[:, 0:1], tail[:, 1:2], tail[:, 2:3]
    low_row, up_row = tail_t[0:1, :], tail_t[1:2, :]
    m[half:, :half] = packed[:, :half] - low_col * up_row
    right = packed[:, half:width]
    low = right - low_col * low_row
    up = jnp.where(iota((half, half), 0) == iota((half, half), 1), diag, right) - up_col * up_row
    for i in range(0, half, BLOCK):
        keep = iota((BLOCK, BLOCK), 0) >= iota((BLOCK, BLOCK), 1)
        for j in range(0, i + BLOCK, BLOCK):
            block = up[j : j + BLOCK, i : i + BLOCK]
            turned = block.T
            if i == j:
                turned = jnp.where(keep, turned, block)
            m[i : i + BLOCK, j : j + BLOCK] = turned
            block = low[i : i + BLOCK, j : j + BLOCK]
            if i == j:
                block = jnp.where(keep, block, block.T)
            m[half + i : half + i + BLOCK, half + j : half + j + BLOCK] = block
    for b in range(0, width, BLOCK):
        after = b + BLOCK
        g[...] = m[b:after, b:after]
        diag_factor(g, wd)
        wk = wd[...]
        w[b:after, b:after] = wk
        if b:
            w[b:after, :b] = dot3(wk, m[b:after, :b], NN)
        if after < width:
            lk = dot3(m[after:, b:after], wk, NT)
            m[after:, b:after] = jnp.zeros((width - after, BLOCK), F32)
            m[after:, :after] = m[after:, :after] - dot3(lk, w[b:after, :after], NN)
            m[after:, after:] = m[after:, after:] - dot3(lk, lk, NT)
    mean = jnp.concatenate([up_row, low_row], 1)
    centred = x_ref[...] - mean
    step = 256
    for j in range(0, width, step):
        if j + step < width:
            w[j : j + BLOCK, j + BLOCK : j + step] = jnp.zeros((BLOCK, step - BLOCK), F32)
        else:
            w[j : j + BLOCK, j + BLOCK :] = jnp.zeros((BLOCK, width - j - BLOCK), F32)
        white_ref[:, j : j + step] = dot3(
            centred[:, : j + step], w[j : j + step, : j + step], NT
        ).astype(BF16)


def whiten(count, core, mine, other, x):
    width = x.shape[1]
    half = width // 2
    vmem = pl.BlockSpec(memory_space=pltpu.VMEM)
    return pl.pallas_call(
        functools.partial(whiten_kernel, count),
        out_shape=jax.ShapeDtypeStruct(x.shape, BF16),
        in_specs=[pl.BlockSpec(memory_space=pltpu.SMEM), vmem, vmem, vmem],
        out_specs=vmem,
        scratch_shapes=[
            pltpu.VMEM((half, width + EXTRA), F32),
            pltpu.VMEM((width, width), F32),
            pltpu.VMEM((width, width), F32),
            pltpu.VMEM((BLOCK, BLOCK), F32),
            pltpu.VMEM((BLOCK, BLOCK), F32),
        ],
        compiler_params=pltpu.CompilerParams(vmem_limit_bytes=VMEM),
        name="whiten",
    )(core, mine, other, x)


def terms_kernel(rows, first, last, n_queries, n_keys, *refs):
    q_refs, refs = refs[:n_queries], refs[n_queries:]
    key_refs, refs = refs[:n_keys], refs[n_keys:]
    if first:
        numer_in = stat_in = None
    else:
        numer_in, stat_in, refs = refs[0], refs[1], refs[2:]
    if last:
        outs, refs = refs[:-1], refs[-1:]
        keys = refs[0]
    else:
        numer_out, stat_out, keys = refs
    q = jnp.concatenate([ref[...] for ref in q_refs], 0)
    queries, width = q.shape
    rate = SHARPNESS / width * math.log2(math.e)
    if first:
        qf = q.astype(F32)
        q_term = 2.0 * SHARPNESS * math.log2(math.e) - rate * jnp.sum(qf * qf, axis=1, keepdims=True)
        total = jnp.zeros((queries, 1), F32)
    else:
        q_term, total = stat_in[:, 0:1], stat_in[:, 1:2]
    place = 0
    for ref in key_refs:
        size = ref.shape[0]
        keys[place : place + size, :] = ref[...]
        place += size
    k = keys[...]
    kf = k.astype(F32)
    k_sq = jnp.sum(kf * kf, axis=1, keepdims=True)
    k_row = jnp.concatenate(
        [jnp.broadcast_to(k_sq[j : j + 128], (128, 128)).T[0:1, :] for j in range(0, place, 128)], 1
    )
    step = 384
    terms = []
    for j in range(0, place, step):
        kern = jnp.exp2(
            q_term - rate * k_row[:, j : j + step] + (2.0 * rate) * mul(q, k[j : j + step], NT)
        )
        if first and j == 0:
            own = (iota(kern.shape, 0) == iota(kern.shape, 1)) & (
                iota(kern.shape, 1) < rows
            )
            kern = jnp.where(own, 0.0, kern)
        total = total + jnp.sum(kern, axis=1, keepdims=True)
        terms.append(kern.astype(BF16))
    numer = mul(jnp.concatenate(terms, 1), k, NN)
    if not first:
        numer = numer_in[...] + numer
    if not last:
        numer_out[...] = numer
        lane = iota((queries, EXTRA), 1)
        stat_out[...] = jnp.where(lane == 0, q_term, total)
        return
    lane = iota((queries, EXTRA), 1)
    hi, lo = split(total)
    wide = jnp.where(lane == 0, hi.astype(F32), jnp.where(lane == 1, lo.astype(F32), 0.0))
    for i, out in enumerate(outs):
        out[:, :width] = numer[i * rows : (i + 1) * rows].astype(BF16)
        out[:, width:] = wide[i * rows : (i + 1) * rows].astype(BF16)


def moves(row_count):
    return [(dy, dx) for dy in range(row_count // 2) for dx in range(2)]


def turn(row, dy, dx, row_count):
    y, x = row // 2, row % 2
    return (y + dy) % (row_count // 2) * 2 + (x + dx) % 2


def terms(rows, query_list, key_list, state, last):
    width = query_list[0].shape[1]
    queries = sum(q.shape[0] for q in query_list)
    n_keys = len(key_list)
    keys = sum(k.shape[0] for k in key_list)
    vmem = pl.BlockSpec(memory_space=pltpu.VMEM)
    if last:
        out_shape = (jax.ShapeDtypeStruct((rows, width + EXTRA), BF16),) * (queries // rows)
    else:
        out_shape = (
            jax.ShapeDtypeStruct((queries, width), F32),
            jax.ShapeDtypeStruct((queries, EXTRA), F32),
        )
    return pl.pallas_call(
        functools.partial(terms_kernel, rows, not state, last, len(query_list), n_keys),
        out_shape=out_shape,
        in_specs=[vmem] * (len(query_list) + n_keys + len(state)),
        out_specs=(vmem,) * len(out_shape),
        scratch_shapes=[pltpu.VMEM((keys, width), BF16)],
        compiler_params=pltpu.CompilerParams(vmem_limit_bytes=TERMS_VMEM),
        cost_estimate=pl.CostEstimate(
            flops=4 * queries * keys * width,
            bytes_accessed=8 * queries * width,
            transcendentals=queries * keys,
        ),
        name="terms",
    )(*query_list, *key_list, *state)


def shift(sizes, dx=0, dz=0, dc=0):
    rows, his, zs = sizes
    pairs = []
    for r in range(rows):
        for h in range(his):
            for z in range(zs):
                for c in range(2):
                    src = ((r * his + h) * zs + z) * 2 + c
                    dst = ((r * his + (h + dx) % his) * zs + (z + dz) % zs) * 2 + (c ^ dc)
                    pairs.append((src, dst))
    return pairs


def shards(embeddings):
    rows, width = embeddings.shape
    row_count = lax.axis_size("row")
    col_count = lax.axis_size("col")
    count = rows * row_count * col_count
    core = (lax.axis_index("col") % 2).astype(jnp.int32)[None]
    his, zs = 2, col_count // 4
    sizes = (row_count, his, zs)
    half = col_count // 2
    groups = [[2 * i + c for i in range(half)] for c in range(2)]
    send = functools.partial(lax.ppermute, axis_name=AXES)
    to_core = shift(sizes, dc=1)

    mine = moments(core, embeddings, send(embeddings, perm=to_core))
    wide = mine.shape[1]
    mine = lax.all_to_all(mine.reshape(row_count, -1, wide), "row", 0, 0).sum(0)
    mine = lax.all_to_all(
        mine.reshape(half, -1, wide), "col", 0, 0, axis_index_groups=groups
    ).sum(0)
    mine = lax.all_to_all(
        jnp.broadcast_to(mine[None], (half,) + mine.shape), "col", 0, 0, axis_index_groups=groups
    ).reshape(-1, wide)
    mine = lax.all_to_all(
        jnp.broadcast_to(mine[None], (row_count,) + mine.shape), "row", 0, 0
    ).reshape(-1, wide)
    other = send(mine, perm=to_core)
    white = whiten(count, core, mine, other, embeddings)

    def row_shift(dy, dx, back):
        pairs = []
        for r in range(row_count):
            for c in range(col_count):
                ends = (r * col_count + c, turn(r, dy, dx, row_count) * col_count + c)
                pairs.append(ends[::-1] if back else ends)
        return pairs

    far = send(white, perm=shift(sizes, dx=1))
    near = send(white, perm=row_shift(0, 1, True))
    pair = jnp.concatenate([white, far], 0)
    asked = jnp.concatenate([white, near], 0)
    queries = [asked] + [
        send(asked, perm=row_shift(dy, 0, True)) for dy in range(1, row_count // 2)
    ]
    right = left = pair
    up, down = shift(sizes, dz=1), shift(sizes, dz=-1)
    arrived = []
    for _ in range((zs - 1) // 2):
        right = send(right, perm=up)
        left = send(left, perm=down)
        arrived.append([right, left])
    if zs % 2 == 0:
        arrived[-1] += [send(right[:rows], perm=up), send(left[rows:], perm=down)]
    arrived[0] = [pair] + arrived[0]
    state = ()
    for i, blocks in enumerate(arrived):
        blocks = blocks + [send(block, perm=to_core) for block in blocks]
        state = terms(rows, queries, blocks, state, i == len(arrived) - 1)
    sums = state[0].astype(F32)
    for (dy, dx), part in list(zip(moves(row_count), state))[1:]:
        sums = sums + send(part, perm=row_shift(dy, dx, False)).astype(F32)
    total = sums[:, width] + sums[:, width + 1]
    smoothed = sums[:, :width] / total[:, None]
    log_density = jnp.log(total / (count - 1))
    return (smoothed, log_density)


def solution(mesh):
    in_specs = (P(("col", "row"), None),)
    out_specs = (P(("col", "row"), None), P(("col", "row")))
    return jax.shard_map(shards, mesh=mesh, in_specs=in_specs, out_specs=out_specs, check_vma=False)
```

```python
import functools
import math
import jax
import jax.numpy as jnp
from jax import lax
from jax.experimental import pallas as pl
from jax.experimental.pallas import tpu as pltpu
from jax.sharding import PartitionSpec as P

SHARPNESS = 24.0
BLOCK = 128
PANEL = 16
EXTRA = 128
STRIP = 256
VMEM = 56 * 2**20
SOME_VMEM = 40 * 2**20
AXES = ("row", "col")
NN = ((1,), (0,))
NT = ((1,), (1,))
BF16 = jnp.bfloat16
F32 = jnp.float32


def split(a):
    hi = a.astype(BF16)
    return hi, (a - hi.astype(F32)).astype(BF16)


def mul(a, b, dims):
    return lax.dot_general(a, b, (dims, ((), ())), preferred_element_type=F32)


def dot3(a, b, dims):
    a_hi, a_lo = split(a)
    b_hi, b_lo = split(b)
    return mul(a_hi, b_hi, dims) + (mul(a_hi, b_lo, dims) + mul(a_lo, b_hi, dims))


def iota(shape, dim):
    return lax.broadcasted_iota(jnp.int32, shape, dim)


def moments_kernel(core_ref, x_ref, y_ref, out_ref, turned_hi, turned_lo):
    rows, width = x_ref.shape
    half = width // 2
    part = half // 2
    pad = jnp.zeros((BLOCK - rows, width), F32)
    x = jnp.concatenate([x_ref[...], pad, y_ref[...], pad], 0)
    hi, lo = split(x)
    for c in range(0, width, BLOCK):
        t_hi, t_lo = split(x[:, c : c + BLOCK].T)
        turned_hi[c : c + BLOCK, :] = t_hi
        turned_lo[c : c + BLOCK, :] = t_lo
    core = core_ref[0]

    def product(start, right_hi, right_lo):
        place = pl.ds(pl.multiple_of(start + core * part, part), part)
        left_hi, left_lo = turned_hi[place, :], turned_lo[place, :]
        small = mul(left_lo, right_lo, NN)
        small = small + (mul(left_hi, right_lo, NN) + mul(left_lo, right_hi, NN))
        return mul(left_hi, right_hi, NN) + small

    low = product(half, hi, lo)
    up = product(0, hi[:, :half], lo[:, :half])
    ones = jnp.where(iota((2 * BLOCK, EXTRA), 1) == 0, 1.0, 0.0).astype(BF16)
    none = jnp.zeros((2 * BLOCK, EXTRA), BF16)
    low_sum = product(half, ones, none)
    up_sum = product(0, ones, none)
    r, c = iota((part, half), 0) + core * part, iota((part, half), 1)
    diag = jnp.sum(jnp.where(r == c, up, 0.0), axis=1, keepdims=True)
    lane = iota((part, EXTRA), 1)
    out_ref[:, :half] = low[:, :half]
    out_ref[:, half:width] = jnp.where(r >= c, low[:, half:], up)
    out_ref[:, width:] = jnp.where(
        lane == 0,
        low_sum,
        jnp.where(lane == 1, up_sum[:, :1], jnp.where(lane == 2, diag, 0.0)),
    )


def moments(core, x, y):
    width = x.shape[1]
    vmem = pl.BlockSpec(memory_space=pltpu.VMEM)
    return pl.pallas_call(
        moments_kernel,
        out_shape=jax.ShapeDtypeStruct((width // 4, width + EXTRA), F32),
        in_specs=[pl.BlockSpec(memory_space=pltpu.SMEM), vmem, vmem],
        out_specs=vmem,
        scratch_shapes=[pltpu.VMEM((width, 2 * BLOCK), BF16)] * 2,
        compiler_params=pltpu.CompilerParams(vmem_limit_bytes=VMEM),
        name="moments",
    )(core, x, y)


def row_of(v, s):
    return jnp.broadcast_to(v[s : s + 1, :], (PANEL, BLOCK))


def columns_of(v, o):
    return [jnp.broadcast_to(v[:, o + s : o + s + 1], (PANEL, BLOCK)) for s in range(PANEL)]


def diag_factor(g, w):
    lane = iota((PANEL, BLOCK), 1)
    sub = iota((PANEL, BLOCK), 0)
    r = g[:PANEL, :]
    for o in range(0, BLOCK, PANEL):
        after = o + PANEL
        if after < BLOCK:
            ahead = g[after : after + PANEL, :]
            factors = columns_of(ahead, o)
        cols = columns_of(r, o)
        inside = (lane >= o) & (lane < after)
        e = jnp.where(inside, jnp.where(lane - o == sub, 1.0, 0.0), r)
        y = jnp.zeros_like(r)
        for s in range(PANEL):
            d = row_of(cols[s], s)
            inv = 1.0 / d
            pivot = row_of(e, s)
            y = jnp.where(sub == s, pivot * lax.rsqrt(d), y)
            m = jnp.where(sub != s, cols[s] * inv, 1.0 - inv)
            e = e - m * pivot
            for t in range(s + 1, PANEL):
                cols[t] = cols[t] - m * row_of(cols[t], s)
        w[o:after, :] = jnp.where(lane <= sub + o, y, 0.0)
        if after < BLOCK:
            sums = [jnp.zeros_like(r)] * 4
            for s in range(PANEL):
                sums[s % 4] = sums[s % 4] + factors[s] * row_of(e, s)
            r = jnp.where(inside, 0.0, ahead) - ((sums[0] + sums[1]) + (sums[2] + sums[3]))
        far = after + PANEL
        if far < BLOCK:
            rest = g[far:, :]
            place = iota(rest.shape, 1)
            inside = (place >= o) & (place < after)
            parts = [e, jnp.zeros((BLOCK - after, BLOCK), F32)]
            if o:
                parts = [jnp.zeros((o, BLOCK), F32)] + parts
            z = jnp.concatenate(parts, 0)
            g[far:, :] = jnp.where(inside, 0.0, rest) - dot3(jnp.where(inside, rest, 0.0), z, NN)


def whiten_kernel(
    count, core_ref, mine_ref, other_ref, x_ref, white_ref, packed, m, w, g, wd
):
    width = x_ref.shape[1]
    half = width // 2
    part = half // 2
    core = core_ref[0]
    scale = 1.0 / count
    packed[pl.ds(pl.multiple_of(core * part, part), part), :] = mine_ref[...] * scale
    packed[pl.ds(pl.multiple_of((1 - core) * part, part), part), :] = other_ref[...] * scale
    tail = packed[:, width:]
    tail_t = tail.T
    low_col, up_col, diag = tail[:, 0:1], tail[:, 1:2], tail[:, 2:3]
    low_row, up_row = tail_t[0:1, :], tail_t[1:2, :]
    m[half:, :half] = packed[:, :half] - low_col * up_row
    right = packed[:, half:width]
    low = right - low_col * low_row
    up = jnp.where(iota((half, half), 0) == iota((half, half), 1), diag, right) - up_col * up_row
    for i in range(0, half, BLOCK):
        keep = iota((BLOCK, BLOCK), 0) >= iota((BLOCK, BLOCK), 1)
        for j in range(0, i + BLOCK, BLOCK):
            block = up[j : j + BLOCK, i : i + BLOCK]
            turned = block.T
            if i == j:
                turned = jnp.where(keep, turned, block)
            m[i : i + BLOCK, j : j + BLOCK] = turned
            block = low[i : i + BLOCK, j : j + BLOCK]
            if i == j:
                block = jnp.where(keep, block, block.T)
            m[half + i : half + i + BLOCK, half + j : half + j + BLOCK] = block
    for b in range(0, width, BLOCK):
        after = b + BLOCK
        g[...] = m[b:after, b:after]
        diag_factor(g, wd)
        wk = wd[...]
        w[b:after, b:after] = wk
        if b:
            w[b:after, :b] = dot3(wk, m[b:after, :b], NN)
        if after < width:
            lk = dot3(m[after:, b:after], wk, NT)
            lk_hi, lk_lo = split(lk)
            both = jnp.concatenate([lk_hi, lk_lo], 1)
            twice = jnp.concatenate([lk_hi, lk_hi], 1)
            w_hi, w_lo = split(w[b:after, :after])
            left = mul(both, jnp.concatenate([w_hi, w_hi], 0), NN) + mul(lk_hi, w_lo, NN)
            if b:
                m[after:, :b] = m[after:, :b] - left[:, :b]
            m[after:, b:after] = -left[:, b:]
            for j in range(after, width, STRIP):
                end = min(j + STRIP, width)
                i, n = j - after, end - after
                term = mul(both[i:], twice[i:n], NT) + mul(lk_hi[i:], lk_lo[i:n], NT)
                m[j:, j:end] = m[j:, j:end] - term
    mean = jnp.concatenate([up_row, low_row], 1)
    centred = x_ref[...] - mean
    step = 256
    for j in range(0, width, step):
        if j + step < width:
            w[j : j + BLOCK, j + BLOCK : j + step] = jnp.zeros((BLOCK, step - BLOCK), F32)
        else:
            w[j : j + BLOCK, j + BLOCK :] = jnp.zeros((BLOCK, width - j - BLOCK), F32)
        white_ref[:, j : j + step] = dot3(
            centred[:, : j + step], w[j : j + step, : j + step], NT
        ).astype(BF16)


def whiten(count, core, mine, other, x):
    width = x.shape[1]
    half = width // 2
    vmem = pl.BlockSpec(memory_space=pltpu.VMEM)
    return pl.pallas_call(
        functools.partial(whiten_kernel, count),
        out_shape=jax.ShapeDtypeStruct(x.shape, BF16),
        in_specs=[pl.BlockSpec(memory_space=pltpu.SMEM), vmem, vmem, vmem],
        out_specs=vmem,
        scratch_shapes=[
            pltpu.VMEM((half, width + EXTRA), F32),
            pltpu.VMEM((width, width), F32),
            pltpu.VMEM((width, width), F32),
            pltpu.VMEM((BLOCK, BLOCK), F32),
            pltpu.VMEM((BLOCK, BLOCK), F32),
        ],
        compiler_params=pltpu.CompilerParams(vmem_limit_bytes=SOME_VMEM),
        name="whiten",
    )(core, mine, other, x)


def terms_kernel(rows, first, last, n_queries, n_keys, *refs):
    q_refs, refs = refs[:n_queries], refs[n_queries:]
    key_refs, refs = refs[:n_keys], refs[n_keys:]
    if first:
        numer_in = stat_in = None
    else:
        numer_in, stat_in, refs = refs[0], refs[1], refs[2:]
    if last:
        outs, refs = refs[:-1], refs[-1:]
        keys = refs[0]
    else:
        numer_out, stat_out, keys = refs
    q = jnp.concatenate([ref[...] for ref in q_refs], 0)
    queries, width = q.shape
    rate = SHARPNESS / width * math.log2(math.e)
    if first:
        qf = q.astype(F32)
        q_term = 2.0 * SHARPNESS * math.log2(math.e) - rate * jnp.sum(qf * qf, axis=1, keepdims=True)
        total = jnp.zeros((queries, 1), F32)
    else:
        q_term, total = stat_in[:, 0:1], stat_in[:, 1:2]
    place = 0
    for ref in key_refs:
        size = ref.shape[0]
        keys[place : place + size, :] = ref[...]
        place += size
    k = keys[...]
    kf = k.astype(F32)
    k_sq = jnp.sum(kf * kf, axis=1, keepdims=True)
    k_row = jnp.concatenate(
        [jnp.broadcast_to(k_sq[j : j + 128], (128, 128)).T[0:1, :] for j in range(0, place, 128)], 1
    )
    step = 384
    terms = []
    for j in range(0, place, step):
        kern = jnp.exp2(
            q_term - rate * k_row[:, j : j + step] + (2.0 * rate) * mul(q, k[j : j + step], NT)
        )
        if first and j == 0:
            own = (iota(kern.shape, 0) == iota(kern.shape, 1)) & (
                iota(kern.shape, 1) < rows
            )
            kern = jnp.where(own, 0.0, kern)
        total = total + jnp.sum(kern, axis=1, keepdims=True)
        terms.append(kern.astype(BF16))
    numer = mul(jnp.concatenate(terms, 1), k, NN)
    if not first:
        numer = numer_in[...] + numer
    if not last:
        numer_out[...] = numer
        lane = iota((queries, EXTRA), 1)
        stat_out[...] = jnp.where(lane == 0, q_term, total)
        return
    lane = iota((queries, EXTRA), 1)
    hi, lo = split(total)
    wide = jnp.where(lane == 0, hi.astype(F32), jnp.where(lane == 1, lo.astype(F32), 0.0))
    for i, out in enumerate(outs):
        out[:, :width] = numer[i * rows : (i + 1) * rows].astype(BF16)
        out[:, width:] = wide[i * rows : (i + 1) * rows].astype(BF16)


def moves(row_count):
    return [(dy, dx) for dy in range(row_count // 2) for dx in range(2)]


def turn(row, dy, dx, row_count):
    y, x = row // 2, row % 2
    return (y + dy) % (row_count // 2) * 2 + (x + dx) % 2


def terms(rows, query_list, key_list, state, last):
    width = query_list[0].shape[1]
    queries = sum(q.shape[0] for q in query_list)
    n_keys = len(key_list)
    keys = sum(k.shape[0] for k in key_list)
    vmem = pl.BlockSpec(memory_space=pltpu.VMEM)
    if last:
        out_shape = (jax.ShapeDtypeStruct((rows, width + EXTRA), BF16),) * (queries // rows)
    else:
        out_shape = (
            jax.ShapeDtypeStruct((queries, width), F32),
            jax.ShapeDtypeStruct((queries, EXTRA), F32),
        )
    return pl.pallas_call(
        functools.partial(terms_kernel, rows, not state, last, len(query_list), n_keys),
        out_shape=out_shape,
        in_specs=[vmem] * (len(query_list) + n_keys + len(state)),
        out_specs=(vmem,) * len(out_shape),
        scratch_shapes=[pltpu.VMEM((keys, width), BF16)],
        compiler_params=pltpu.CompilerParams(vmem_limit_bytes=SOME_VMEM),
        cost_estimate=pl.CostEstimate(
            flops=4 * queries * keys * width,
            bytes_accessed=8 * queries * width,
            transcendentals=queries * keys,
        ),
        name="terms",
    )(*query_list, *key_list, *state)


def shift(sizes, dx=0, dz=0, dc=0):
    rows, his, zs = sizes
    pairs = []
    for r in range(rows):
        for h in range(his):
            for z in range(zs):
                for c in range(2):
                    src = ((r * his + h) * zs + z) * 2 + c
                    dst = ((r * his + (h + dx) % his) * zs + (z + dz) % zs) * 2 + (c ^ dc)
                    pairs.append((src, dst))
    return pairs


def shards(embeddings):
    rows, width = embeddings.shape
    row_count = lax.axis_size("row")
    col_count = lax.axis_size("col")
    count = rows * row_count * col_count
    core = (lax.axis_index("col") % 2).astype(jnp.int32)[None]
    his, zs = 2, col_count // 4
    sizes = (row_count, his, zs)
    half = col_count // 2
    groups = [[2 * i + c for i in range(half)] for c in range(2)]
    send = functools.partial(lax.ppermute, axis_name=AXES)
    to_core = shift(sizes, dc=1)

    mine = moments(core, embeddings, send(embeddings, perm=to_core))
    wide = mine.shape[1]
    mine = lax.all_to_all(mine.reshape(row_count, -1, wide), "row", 0, 0).sum(0)
    mine = lax.all_to_all(
        mine.reshape(half, -1, wide), "col", 0, 0, axis_index_groups=groups
    ).sum(0)
    mine = lax.all_to_all(
        jnp.broadcast_to(mine[None], (half,) + mine.shape), "col", 0, 0, axis_index_groups=groups
    ).reshape(-1, wide)
    mine = lax.all_to_all(
        jnp.broadcast_to(mine[None], (row_count,) + mine.shape), "row", 0, 0
    ).reshape(-1, wide)
    other = send(mine, perm=to_core)
    white = whiten(count, core, mine, other, embeddings)

    def row_shift(dy, dx, back):
        pairs = []
        for r in range(row_count):
            for c in range(col_count):
                ends = (r * col_count + c, turn(r, dy, dx, row_count) * col_count + c)
                pairs.append(ends[::-1] if back else ends)
        return pairs

    far = send(white, perm=shift(sizes, dx=1))
    pair = jnp.concatenate([white, far], 0)
    pair, later = lax.optimization_barrier((pair, white))
    near = send(later, perm=row_shift(0, 1, True))
    asked = jnp.concatenate([white, near], 0)
    queries = [asked] + [
        send(asked, perm=row_shift(dy, 0, True)) for dy in range(1, row_count // 2)
    ]
    right = left = pair
    up, down = shift(sizes, dz=1), shift(sizes, dz=-1)
    arrived = []
    for _ in range((zs - 1) // 2):
        right = send(right, perm=up)
        left = send(left, perm=down)
        arrived.append([right, left])
    if zs % 2 == 0:
        arrived[-1] += [send(right[:rows], perm=up), send(left[rows:], perm=down)]
    arrived[0] = [pair] + arrived[0]
    state = ()
    for i, blocks in enumerate(arrived):
        blocks = blocks + [send(block, perm=to_core) for block in blocks]
        state = terms(rows, queries, blocks, state, i == len(arrived) - 1)
    sums = state[0].astype(F32)
    tail = list(zip(moves(row_count), state))[1:]
    for (dy, dx), part in sorted(tail, key=lambda item: -item[0][1]):
        sums = sums + send(part, perm=row_shift(dy, dx, False)).astype(F32)
    total = sums[:, width] + sums[:, width + 1]
    smoothed = sums[:, :width] / total[:, None]
    log_density = jnp.log(total / (count - 1))
    return (smoothed, log_density)


def solution(mesh):
    in_specs = (P(("col", "row"), None),)
    out_specs = (P(("col", "row"), None), P(("col", "row")))
    return jax.shard_map(shards, mesh=mesh, in_specs=in_specs, out_specs=out_specs, check_vma=False)
```

```python
import functools
import math
import jax
import jax.numpy as jnp
from jax import lax
from jax.experimental import pallas as pl
from jax.experimental.pallas import tpu as pltpu
from jax.sharding import PartitionSpec as P

SHARPNESS = 24.0
BLOCK = 128
PANEL = 16
EXTRA = 128
STRIP = 256
VMEM = 56 * 2**20
SOME_VMEM = 40 * 2**20
AXES = ("row", "col")
NN = ((1,), (0,))
NT = ((1,), (1,))
BF16 = jnp.bfloat16
F32 = jnp.float32


def split(a):
    hi = a.astype(BF16)
    return hi, (a - hi.astype(F32)).astype(BF16)


def mul(a, b, dims):
    return lax.dot_general(a, b, (dims, ((), ())), preferred_element_type=F32)


def dot3(a, b, dims):
    a_hi, a_lo = split(a)
    b_hi, b_lo = split(b)
    return mul(a_hi, b_hi, dims) + (mul(a_hi, b_lo, dims) + mul(a_lo, b_hi, dims))


def iota(shape, dim):
    return lax.broadcasted_iota(jnp.int32, shape, dim)


def moments_kernel(core_ref, x_ref, y_ref, out_ref, turned_hi, turned_lo):
    rows, width = x_ref.shape
    half = width // 2
    part = half // 2
    pad = jnp.zeros((BLOCK - rows, width), F32)
    x = jnp.concatenate([x_ref[...], pad, y_ref[...], pad], 0)
    hi, lo = split(x)
    for c in range(0, width, BLOCK):
        t_hi, t_lo = split(x[:, c : c + BLOCK].T)
        turned_hi[c : c + BLOCK, :] = t_hi
        turned_lo[c : c + BLOCK, :] = t_lo
    core = core_ref[0]

    def product(start, right_hi, right_lo):
        place = pl.ds(pl.multiple_of(start + core * part, part), part)
        left_hi, left_lo = turned_hi[place, :], turned_lo[place, :]
        small = mul(left_lo, right_lo, NN)
        small = small + (mul(left_hi, right_lo, NN) + mul(left_lo, right_hi, NN))
        return mul(left_hi, right_hi, NN) + small

    low = product(half, hi, lo)
    up = product(0, hi[:, :half], lo[:, :half])
    ones = jnp.where(iota((2 * BLOCK, EXTRA), 1) == 0, 1.0, 0.0).astype(BF16)
    none = jnp.zeros((2 * BLOCK, EXTRA), BF16)
    low_sum = product(half, ones, none)
    up_sum = product(0, ones, none)
    r, c = iota((part, half), 0) + core * part, iota((part, half), 1)
    diag = jnp.sum(jnp.where(r == c, up, 0.0), axis=1, keepdims=True)
    lane = iota((part, EXTRA), 1)
    out_ref[:, :half] = low[:, :half]
    out_ref[:, half:width] = jnp.where(r >= c, low[:, half:], up)
    out_ref[:, width:] = jnp.where(
        lane == 0,
        low_sum,
        jnp.where(lane == 1, up_sum[:, :1], jnp.where(lane == 2, diag, 0.0)),
    )


def moments(core, x, y):
    width = x.shape[1]
    vmem = pl.BlockSpec(memory_space=pltpu.VMEM)
    return pl.pallas_call(
        moments_kernel,
        out_shape=jax.ShapeDtypeStruct((width // 4, width + EXTRA), F32),
        in_specs=[pl.BlockSpec(memory_space=pltpu.SMEM), vmem, vmem],
        out_specs=vmem,
        scratch_shapes=[pltpu.VMEM((width, 2 * BLOCK), BF16)] * 2,
        compiler_params=pltpu.CompilerParams(vmem_limit_bytes=VMEM),
        name="moments",
    )(core, x, y)


def row_of(v, s):
    return jnp.broadcast_to(v[s : s + 1, :], (PANEL, BLOCK))


def columns_of(v, o):
    return [jnp.broadcast_to(v[:, o + s : o + s + 1], (PANEL, BLOCK)) for s in range(PANEL)]


def diag_factor(g, w):
    lane = iota((PANEL, BLOCK), 1)
    sub = iota((PANEL, BLOCK), 0)
    r = g[:PANEL, :]
    for o in range(0, BLOCK, PANEL):
        after = o + PANEL
        if after < BLOCK:
            ahead = g[after : after + PANEL, :]
            factors = columns_of(ahead, o)
        cols = columns_of(r, o)
        inside = (lane >= o) & (lane < after)
        e = jnp.where(inside, jnp.where(lane - o == sub, 1.0, 0.0), r)
        y = jnp.zeros_like(r)
        for s in range(PANEL):
            d = row_of(cols[s], s)
            inv = 1.0 / d
            pivot = row_of(e, s)
            y = jnp.where(sub == s, pivot * lax.rsqrt(d), y)
            m = jnp.where(sub != s, cols[s] * inv, 1.0 - inv)
            e = e - m * pivot
            for t in range(s + 1, PANEL):
                cols[t] = cols[t] - m * row_of(cols[t], s)
        w[o:after, :] = jnp.where(lane <= sub + o, y, 0.0)
        if after < BLOCK:
            sums = [jnp.zeros_like(r)] * 4
            for s in range(PANEL):
                sums[s % 4] = sums[s % 4] + factors[s] * row_of(e, s)
            r = jnp.where(inside, 0.0, ahead) - ((sums[0] + sums[1]) + (sums[2] + sums[3]))
        far = after + PANEL
        if far < BLOCK:
            rest = g[far:, :]
            place = iota(rest.shape, 1)
            inside = (place >= o) & (place < after)
            parts = [e, jnp.zeros((BLOCK - after, BLOCK), F32)]
            if o:
                parts = [jnp.zeros((o, BLOCK), F32)] + parts
            z = jnp.concatenate(parts, 0)
            g[far:, :] = jnp.where(inside, 0.0, rest) - dot3(jnp.where(inside, rest, 0.0), z, NN)


def whiten_kernel(
    count, core_ref, mine_ref, other_ref, x_ref, white_ref, packed, m, w, g, wd
):
    width = x_ref.shape[1]
    half = width // 2
    part = half // 2
    core = core_ref[0]
    scale = 1.0 / count
    packed[pl.ds(pl.multiple_of(core * part, part), part), :] = mine_ref[...] * scale
    packed[pl.ds(pl.multiple_of((1 - core) * part, part), part), :] = other_ref[...] * scale
    tail = packed[:, width:]
    tail_t = tail.T
    low_col, up_col, diag = tail[:, 0:1], tail[:, 1:2], tail[:, 2:3]
    low_row, up_row = tail_t[0:1, :], tail_t[1:2, :]
    m[half:, :half] = packed[:, :half] - low_col * up_row
    right = packed[:, half:width]
    low = right - low_col * low_row
    up = jnp.where(iota((half, half), 0) == iota((half, half), 1), diag, right) - up_col * up_row
    for i in range(0, half, BLOCK):
        keep = iota((BLOCK, BLOCK), 0) >= iota((BLOCK, BLOCK), 1)
        for j in range(0, i + BLOCK, BLOCK):
            block = up[j : j + BLOCK, i : i + BLOCK]
            turned = block.T
            if i == j:
                turned = jnp.where(keep, turned, block)
            m[i : i + BLOCK, j : j + BLOCK] = turned
            block = low[i : i + BLOCK, j : j + BLOCK]
            if i == j:
                block = jnp.where(keep, block, block.T)
            m[half + i : half + i + BLOCK, half + j : half + j + BLOCK] = block
    for b in range(0, width, BLOCK):
        after = b + BLOCK
        g[...] = m[b:after, b:after]
        diag_factor(g, wd)
        wk = wd[...]
        w[b:after, b:after] = wk
        if b:
            w[b:after, :b] = dot3(wk, m[b:after, :b], NN)
        if after < width:
            lk = dot3(m[after:, b:after], wk, NT)
            lk_hi, lk_lo = split(lk)
            both = jnp.concatenate([lk_hi, lk_lo], 1)
            twice = jnp.concatenate([lk_hi, lk_hi], 1)
            w_hi, w_lo = split(w[b:after, :after])
            left = mul(both, jnp.concatenate([w_hi, w_hi], 0), NN) + mul(lk_hi, w_lo, NN)
            if b:
                m[after:, :b] = m[after:, :b] - left[:, :b]
            m[after:, b:after] = -left[:, b:]
            for j in range(after, width, STRIP):
                end = min(j + STRIP, width)
                i, n = j - after, end - after
                term = mul(both[i:], twice[i:n], NT) + mul(lk_hi[i:], lk_lo[i:n], NT)
                m[j:, j:end] = m[j:, j:end] - term
    mean = jnp.concatenate([up_row, low_row], 1)
    centred = x_ref[...] - mean
    step = 256
    for j in range(0, width, step):
        if j + step < width:
            w[j : j + BLOCK, j + BLOCK : j + step] = jnp.zeros((BLOCK, step - BLOCK), F32)
        else:
            w[j : j + BLOCK, j + BLOCK :] = jnp.zeros((BLOCK, width - j - BLOCK), F32)
        white_ref[:, j : j + step] = dot3(
            centred[:, : j + step], w[j : j + step, : j + step], NT
        ).astype(BF16)


def whiten(count, core, mine, other, x):
    width = x.shape[1]
    half = width // 2
    vmem = pl.BlockSpec(memory_space=pltpu.VMEM)
    return pl.pallas_call(
        functools.partial(whiten_kernel, count),
        out_shape=jax.ShapeDtypeStruct(x.shape, BF16),
        in_specs=[pl.BlockSpec(memory_space=pltpu.SMEM), vmem, vmem, vmem],
        out_specs=vmem,
        scratch_shapes=[
            pltpu.VMEM((half, width + EXTRA), F32),
            pltpu.VMEM((width, width), F32),
            pltpu.VMEM((width, width), F32),
            pltpu.VMEM((BLOCK, BLOCK), F32),
            pltpu.VMEM((BLOCK, BLOCK), F32),
        ],
        compiler_params=pltpu.CompilerParams(vmem_limit_bytes=SOME_VMEM),
        name="whiten",
    )(core, mine, other, x)


def terms_kernel(rows, first, last, n_queries, n_keys, *refs):
    q_refs, refs = refs[:n_queries], refs[n_queries:]
    key_refs, refs = refs[:n_keys], refs[n_keys:]
    if first:
        numer_in = stat_in = None
    else:
        numer_in, stat_in, refs = refs[0], refs[1], refs[2:]
    if last:
        outs, refs = refs[:-1], refs[-1:]
        keys = refs[0]
    else:
        numer_out, stat_out, keys = refs
    q = jnp.concatenate([ref[...] for ref in q_refs], 0)
    queries, width = q.shape
    rate = SHARPNESS / width * math.log2(math.e)
    if first:
        qf = q.astype(F32)
        q_term = 2.0 * SHARPNESS * math.log2(math.e) - rate * jnp.sum(qf * qf, axis=1, keepdims=True)
        total = jnp.zeros((queries, 1), F32)
    else:
        q_term, total = stat_in[:, 0:1], stat_in[:, 1:2]
    place = 0
    for ref in key_refs:
        size = ref.shape[0]
        keys[place : place + size, :] = ref[...]
        place += size
    k = keys[...]
    kf = k.astype(F32)
    k_sq = jnp.sum(kf * kf, axis=1, keepdims=True)
    k_row = jnp.concatenate(
        [jnp.broadcast_to(k_sq[j : j + 128], (128, 128)).T[0:1, :] for j in range(0, place, 128)], 1
    )
    step = 384
    terms = []
    for j in range(0, place, step):
        kern = jnp.exp2(
            q_term - rate * k_row[:, j : j + step] + (2.0 * rate) * mul(q, k[j : j + step], NT)
        )
        if first and j == 0:
            own = (iota(kern.shape, 0) == iota(kern.shape, 1)) & (
                iota(kern.shape, 1) < rows
            )
            kern = jnp.where(own, 0.0, kern)
        total = total + jnp.sum(kern, axis=1, keepdims=True)
        terms.append(kern.astype(BF16))
    numer = mul(jnp.concatenate(terms, 1), k, NN)
    if not first:
        numer = numer_in[...] + numer
    if not last:
        numer_out[...] = numer
        lane = iota((queries, EXTRA), 1)
        stat_out[...] = jnp.where(lane == 0, q_term, total)
        return
    lane = iota((queries, EXTRA), 1)
    hi, lo = split(total)
    wide = jnp.where(lane == 0, hi.astype(F32), jnp.where(lane == 1, lo.astype(F32), 0.0))
    for i, out in enumerate(outs):
        out[:, :width] = numer[i * rows : (i + 1) * rows].astype(BF16)
        out[:, width:] = wide[i * rows : (i + 1) * rows].astype(BF16)


def moves(row_count):
    return [(dy, dx) for dy in range(row_count // 2) for dx in range(2)]


def turn(row, dy, dx, row_count):
    y, x = row // 2, row % 2
    return (y + dy) % (row_count // 2) * 2 + (x + dx) % 2


def terms(rows, query_list, key_list, state, last):
    width = query_list[0].shape[1]
    queries = sum(q.shape[0] for q in query_list)
    n_keys = len(key_list)
    keys = sum(k.shape[0] for k in key_list)
    vmem = pl.BlockSpec(memory_space=pltpu.VMEM)
    if last:
        out_shape = (jax.ShapeDtypeStruct((rows, width + EXTRA), BF16),) * (queries // rows)
    else:
        out_shape = (
            jax.ShapeDtypeStruct((queries, width), F32),
            jax.ShapeDtypeStruct((queries, EXTRA), F32),
        )
    return pl.pallas_call(
        functools.partial(terms_kernel, rows, not state, last, len(query_list), n_keys),
        out_shape=out_shape,
        in_specs=[vmem] * (len(query_list) + n_keys + len(state)),
        out_specs=(vmem,) * len(out_shape),
        scratch_shapes=[pltpu.VMEM((keys, width), BF16)],
        compiler_params=pltpu.CompilerParams(vmem_limit_bytes=SOME_VMEM),
        cost_estimate=pl.CostEstimate(
            flops=4 * queries * keys * width,
            bytes_accessed=8 * queries * width,
            transcendentals=queries * keys,
        ),
        name="terms",
    )(*query_list, *key_list, *state)


def shift(sizes, dx=0, dz=0, dc=0):
    rows, his, zs = sizes
    pairs = []
    for r in range(rows):
        for h in range(his):
            for z in range(zs):
                for c in range(2):
                    src = ((r * his + h) * zs + z) * 2 + c
                    dst = ((r * his + (h + dx) % his) * zs + (z + dz) % zs) * 2 + (c ^ dc)
                    pairs.append((src, dst))
    return pairs


def shards(embeddings):
    rows, width = embeddings.shape
    row_count = lax.axis_size("row")
    col_count = lax.axis_size("col")
    count = rows * row_count * col_count
    core = (lax.axis_index("col") % 2).astype(jnp.int32)[None]
    his, zs = 2, col_count // 4
    sizes = (row_count, his, zs)
    half = col_count // 2
    groups = [[2 * i + c for i in range(half)] for c in range(2)]
    send = functools.partial(lax.ppermute, axis_name=AXES)
    to_core = shift(sizes, dc=1)

    mine = moments(core, embeddings, send(embeddings, perm=to_core))
    wide = mine.shape[1]
    mine = lax.all_to_all(mine.reshape(row_count, -1, wide), "row", 0, 0).sum(0)
    mine = lax.all_to_all(
        mine.reshape(half, -1, wide), "col", 0, 0, axis_index_groups=groups
    ).sum(0)
    mine = lax.all_to_all(
        jnp.broadcast_to(mine[None], (half,) + mine.shape), "col", 0, 0, axis_index_groups=groups
    ).reshape(-1, wide)
    mine = lax.all_to_all(
        jnp.broadcast_to(mine[None], (row_count,) + mine.shape), "row", 0, 0
    ).reshape(-1, wide)
    other = send(mine, perm=to_core)
    white = whiten(count, core, mine, other, embeddings)

    def row_shift(dy, dx, back):
        pairs = []
        for r in range(row_count):
            for c in range(col_count):
                ends = (r * col_count + c, turn(r, dy, dx, row_count) * col_count + c)
                pairs.append(ends[::-1] if back else ends)
        return pairs

    far = send(white, perm=shift(sizes, dx=1))
    ys = row_count // 2
    along = {dy: send(white, perm=row_shift(dy, 0, True)) for dy in {1, ys - 1}}
    pair = jnp.concatenate([white, far], 0)
    pair, later, along = lax.optimization_barrier((pair, white, along))
    near = send(later, perm=row_shift(0, 1, True))
    queries = [white, near]
    for dy in range(1, ys):
        if dy not in along:
            along[dy] = send(later, perm=row_shift(dy, 0, True))
        queries += [along[dy], send(near, perm=row_shift(dy, 0, True))]
    right = left = pair
    up, down = shift(sizes, dz=1), shift(sizes, dz=-1)
    arrived = []
    for _ in range((zs - 1) // 2):
        right = send(right, perm=up)
        left = send(left, perm=down)
        arrived.append([right, left])
    if zs % 2 == 0:
        arrived[-1] += [send(right[:rows], perm=up), send(left[rows:], perm=down)]
    arrived[0] = [pair] + arrived[0]
    state = ()
    for i, blocks in enumerate(arrived):
        blocks = blocks + [send(block, perm=to_core) for block in blocks]
        state = terms(rows, queries, blocks, state, i == len(arrived) - 1)
    sums = state[0].astype(F32)
    tail = list(zip(moves(row_count), state))[1:]
    for (dy, dx), part in sorted(tail, key=lambda item: -item[0][1]):
        sums = sums + send(part, perm=row_shift(dy, dx, False)).astype(F32)
    total = sums[:, width] + sums[:, width + 1]
    smoothed = sums[:, :width] / total[:, None]
    log_density = jnp.log(total / (count - 1))
    return (smoothed, log_density)


def solution(mesh):
    in_specs = (P(("col", "row"), None),)
    out_specs = (P(("col", "row"), None), P(("col", "row")))
    return jax.shard_map(shards, mesh=mesh, in_specs=in_specs, out_specs=out_specs, check_vma=False)
```
